256 devices in a mesh: layer: 4 (over x_hi, core), feat: 64 (over z, y, x_lo).
Axes of the slice: x: 4 (x_hi: 2, x_lo: 2; x = x_hi * 2 + x_lo), y: 4, z: 8, core: 2. Of those that a mesh axis runs over, the one named last changes fastest.
Arguments:
- layer_acts: bfloat16 [4, 512, 576], P('layer', 'feat'), may hold values from -6 to 6
- enc_weight: bfloat16 [4, 576, 131072], P('layer', None, 'feat'), may hold values from -6 to 6
- dec_weight: bfloat16 [4, 131072, 576], P('layer', 'feat'), may hold values from -6 to 6
- enc_bias: float32 [131072], P('feat'), may hold values from -4 to 4
- dec_bias: float32 [4, 576], P('layer'), may hold values from -4 to 4
Outputs:
- enc_step: bfloat16 [4, 576, 131072], P('layer', None, 'feat')
- dec_step: bfloat16 [4, 131072, 576], P('layer', 'feat')
The draws below stay inside these ranges and needn't reach their ends.
All inputs are finite; a program needn't handle non-finite values.
Results may differ from the reference program's by a relative error of at most 0.012.
Values may be sent and summed in bfloat16 or wider, within the bound.
No kernel may reach another device: no remote copies, remote signals or barrier semaphores. Data moves between devices by JAX's collectives and lax.ppermute only.
A program may use at most 64 MiB of HBM per device.

```python
import jax
import jax.numpy as jnp
from jax import lax

D = 576
F_DEV = 2048
TOKENS = 512
LAYERS = 4
FEATURES = 131072


def shard_levels(stream_key, shape, cuts, smallest, high):
    def one(dim, blocks):
        heights = jax.random.uniform(jax.random.fold_in(jax.random.fold_in(stream_key, 6), dim), (blocks,), jnp.float32, smallest / len(cuts), high / len(cuts))
        return jnp.repeat(jnp.exp(heights), shape[dim] // blocks).reshape((-1,) + (1,) * (len(shape) - dim - 1))

    factor_of = one(*cuts[0])
    for cut in cuts[1:]:
        factor_of = factor_of * one(*cut)
    return factor_of


def gaussian(rng, shape, deviation, reach, cuts=(), dtype=jnp.bfloat16):
    gain = shard_levels(rng, shape, cuts, -0.22, 0.18) if cuts else 1.0
    drawn = jax.random.normal(rng, shape, jnp.float32) * deviation * gain
    return jnp.minimum(jnp.maximum(drawn, -reach), reach).astype(dtype)


def setup_inputs(seed: int = 0) -> dict:
    keys = jax.random.split(jax.random.key(seed), 6)
    return {
        "layer_acts": gaussian(keys[0], (LAYERS, TOKENS, D), 1.0, 6.0, ((0, 4), (1, 64))),
        "enc_weight": gaussian(keys[1], (LAYERS, D, FEATURES), 1.0, 6.0, ((0, 4), (2, 64))),
        "dec_weight": gaussian(keys[2], (LAYERS, FEATURES, D), 1.0, 6.0, ((0, 4), (1, 64))),
        "enc_bias": gaussian(keys[3], (FEATURES,), 0.7, 4.0, ((0, 64),), jnp.float32),
        "dec_bias": gaussian(keys[4], (LAYERS, D), 0.7, 4.0, ((0, 4),), jnp.float32),
    }


LEARN_RATE = 4.0


def contract_rows(left, right):
    return lax.dot_general(left, right, (((0,), (0,)), ((), ())), preferred_element_type=jnp.float32)


def reference(layer_acts, enc_weight, dec_weight, enc_bias, dec_bias):
    enc_scale = (LAYERS * D) ** -0.5
    dec_scale = FEATURES ** -0.5
    blocks = FEATURES // F_DEV
    enc_blocks = enc_weight.reshape(LAYERS, D, blocks, F_DEV).transpose(2, 0, 1, 3)
    dec_blocks = dec_weight.reshape(LAYERS, blocks, F_DEV, D).transpose(1, 0, 2, 3)
    bias_blocks = enc_bias.reshape(blocks, F_DEV)

    def encode(enc_block, bias_block):
        running = jnp.zeros((TOKENS, F_DEV), jnp.float32)
        for layer_index in range(LAYERS):
            running = running + jnp.dot(layer_acts[layer_index], enc_block[layer_index], preferred_element_type=jnp.float32)
        return enc_scale * running + bias_block

    def forward(recon, parts):
        enc_block, dec_block, bias_block = parts
        preact = encode(enc_block, bias_block)
        active_b = jnp.maximum(preact, 0.0).astype(jnp.bfloat16)
        decoded = jnp.stack([jnp.dot(active_b, dec_block[layer_index], preferred_element_type=jnp.float32) for layer_index in range(LAYERS)])
        return recon + dec_scale * decoded, None

    recon, unused = lax.scan(forward, jnp.zeros((LAYERS, TOKENS, D), jnp.float32), (enc_blocks, dec_blocks, bias_blocks))
    error_b = (recon + dec_bias[:, None, :] - layer_acts.astype(jnp.float32)).astype(jnp.bfloat16)

    def backward(parts):
        enc_block, dec_block, bias_block = parts
        preact = encode(enc_block, bias_block)
        active_b = jnp.maximum(preact, 0.0).astype(jnp.bfloat16)
        grad_dec = jnp.stack([contract_rows(active_b, error_b[layer_index]) for layer_index in range(LAYERS)])
        grad_act = jnp.zeros((TOKENS, F_DEV), jnp.float32)
        for layer_index in range(LAYERS):
            grad_act = grad_act + dec_scale * lax.dot_general(error_b[layer_index], dec_block[layer_index], (((1,), (1,)), ((), ())), preferred_element_type=jnp.float32)
        grad_pre = jnp.where(preact > 0.0, grad_act, 0.0).astype(jnp.bfloat16)
        grad_enc = jnp.stack([contract_rows(layer_acts[layer_index], grad_pre) for layer_index in range(LAYERS)])
        return (-LEARN_RATE * enc_scale * grad_enc).astype(jnp.bfloat16), (-LEARN_RATE * dec_scale * grad_dec).astype(jnp.bfloat16)

    enc_steps, dec_steps = lax.map(backward, (enc_blocks, dec_blocks, bias_blocks))
    enc_step = enc_steps.transpose(1, 2, 0, 3).reshape(LAYERS, D, FEATURES)
    dec_step = dec_steps.transpose(1, 0, 2, 3).reshape(LAYERS, FEATURES, D)
    return enc_step, dec_step
```

```python
import jax
import jax.numpy as jnp
from jax import lax
from jax.sharding import PartitionSpec as P

LEARN_RATE = 4.0
BF16 = jnp.bfloat16
F32 = jnp.float32
ACROSS_CORES = [(0, 1), (1, 0), (2, 3), (3, 2)]
ACROSS_CHIPS = [(0, 2), (1, 3), (2, 0), (3, 1)]


def to_core(value):
    return lax.ppermute(value, "layer", ACROSS_CORES)


def to_chip(value):
    return lax.ppermute(value, "layer", ACROSS_CHIPS)


def gather_tokens(value):
    blocks = lax.axis_size("feat")
    rows, width = value.shape
    copies = jnp.broadcast_to(value[None], (blocks, rows, width))
    return lax.all_to_all(copies, "feat", 0, 0, tiled=True).reshape(blocks * rows, width)


def rows_of(value, start, count):
    return lax.dynamic_slice_in_dim(value, start, count, axis=0)


def dot(left, right):
    return jnp.dot(left, right, preferred_element_type=F32)


def dot_transposed(left, right):
    return lax.dot_general(left, right, (((1,), (1,)), ((), ())), preferred_element_type=F32)


def contract_rows(left, right):
    return lax.dot_general(left, right, (((0,), (0,)), ((), ())), preferred_element_type=F32)


def body(layer_acts, enc_weight, dec_weight, enc_bias, dec_bias):
    tok_local = layer_acts[0]
    enc_local = enc_weight[0]
    dec_local = dec_weight[0]
    bias = enc_bias[None, :]
    model_width, slab_width = enc_local.shape
    blocks = lax.axis_size("feat")
    enc_scale = (layer_acts.shape[0] * lax.axis_size("layer") * model_width) ** (-0.5)
    dec_scale = (slab_width * blocks) ** (-0.5)
    tokens = tok_local.shape[0] * blocks
    half, quarter = tokens // 2, tokens // 4
    place = lax.axis_index("layer")
    chip, core = place // 2, place % 2

    def quarter_at(core_index, chip_index):
        return core_index * half + chip_index * quarter

    mine = quarter_at(core, chip)
    of_chip = quarter_at(core, 1 - chip)
    of_core = quarter_at(1 - core, chip)
    of_both = quarter_at(1 - core, 1 - chip)

    whole_tokens = gather_tokens(tok_local)

    def encode(start):
        return dot(rows_of(whole_tokens, start, quarter), enc_local)

    sum_of_chip = encode(of_chip) + to_core(encode(of_both))
    arrived = to_chip(sum_of_chip)
    sum_mine = encode(mine) + to_core(encode(of_core))
    preact = enc_scale * (sum_mine + arrived) + bias
    active_mine = jnp.maximum(preact, 0.0).astype(BF16)
    active_of_chip = to_chip(active_mine)
    active_of_core = to_core(active_mine)
    active_of_both = to_core(active_of_chip)

    pieces = (
        (mine, active_mine),
        (of_core, active_of_core),
        (of_chip, active_of_chip),
        (of_both, active_of_both),
    )
    recon_terms = jnp.zeros((tokens, model_width), BF16)
    for start, active in pieces:
        term = (dec_scale * dot(active, dec_local)).astype(BF16)
        recon_terms = lax.dynamic_update_slice_in_dim(recon_terms, term, start, axis=0)
    arrived_terms = lax.all_to_all(
        recon_terms.reshape(blocks, tokens // blocks, model_width), "feat", 0, 0, tiled=True
    )
    recon = jnp.sum(arrived_terms.astype(F32), axis=0)
    error_b = (recon + dec_bias[0] - tok_local.astype(F32)).astype(BF16)
    whole_errors = gather_tokens(error_b)

    def enc_rows(starts):
        return jnp.concatenate([rows_of(whole_tokens, start, quarter) for start in starts])

    own_rows = (mine, of_chip)
    other_rows = (of_core, of_both)
    errors_other = jnp.concatenate([rows_of(whole_errors, start, quarter) for start in other_rows])
    errors_own = jnp.concatenate([rows_of(whole_errors, start, quarter) for start in own_rows])
    grad_other = dot_transposed(errors_other, dec_local).astype(BF16)
    grad_from_core = to_core(grad_other).astype(F32)
    grad_pair = dot_transposed(errors_own, dec_local) + grad_from_core
    grad_pair_b = grad_pair.astype(BF16)
    from_chip = to_chip(grad_pair_b).astype(F32)
    from_chip = jnp.concatenate([from_chip[quarter:], from_chip[:quarter]])
    grad_act = dec_scale * (grad_pair + from_chip)
    active_own = jnp.concatenate([active_mine, active_of_chip])
    grad_pre_own = jnp.where(active_own > 0, grad_act, 0.0).astype(BF16)
    grad_pre_other = to_core(grad_pre_own)

    active_all = jnp.concatenate([active for _, active in pieces])
    errors_all = jnp.concatenate([rows_of(whole_errors, start, quarter) for start, _ in pieces])
    grad_dec = contract_rows(active_all, errors_all)
    grad_enc = contract_rows(enc_rows(own_rows + other_rows), jnp.concatenate([grad_pre_own, grad_pre_other]))
    enc_step = (-LEARN_RATE * enc_scale * grad_enc).astype(BF16)[None]
    dec_step = (-LEARN_RATE * dec_scale * grad_dec).astype(BF16)[None]
    return (enc_step, dec_step)


def solution(mesh):
    in_specs = (
        P("layer", "feat", None),
        P("layer", None, "feat"),
        P("layer", "feat", None),
        P("feat"),
        P("layer", None),
    )
    out_specs = (P("layer", None, "feat"), P("layer", "feat", None))
    return jax.shard_map(body, mesh=mesh, in_specs=in_specs, out_specs=out_specs, check_vma=False)
```

```python
import functools

import jax
import jax.numpy as jnp
from jax import lax
from jax.experimental import pallas as pl
from jax.experimental.pallas import tpu as pltpu
from jax.sharding import PartitionSpec as P

LEARN_RATE = 4.0
BF16 = jnp.bfloat16
F32 = jnp.float32
ACROSS_CORES = [(0, 1), (1, 0), (2, 3), (3, 2)]
ACROSS_CHIPS = [(0, 2), (1, 3), (2, 0), (3, 1)]


def to_core(value):
    return lax.ppermute(value, "layer", ACROSS_CORES)


def to_chip(value):
    return lax.ppermute(value, "layer", ACROSS_CHIPS)


def gather_tokens(value):
    blocks = lax.axis_size("feat")
    rows, width = value.shape
    copies = jnp.broadcast_to(value[None], (blocks, rows, width))
    return lax.all_to_all(copies, "feat", 0, 0, tiled=True).reshape(blocks * rows, width)


def rows_of(value, start, count):
    return lax.dynamic_slice_in_dim(value, start, count, axis=0)


def dot(left, right):
    return jnp.dot(left, right, preferred_element_type=F32)


def dot_transposed(left, right):
    return lax.dot_general(left, right, (((1,), (1,)), ((), ())), preferred_element_type=F32)


def contract_rows(left, right):
    return lax.dot_general(left, right, (((0,), (0,)), ((), ())), preferred_element_type=F32)


def decode_kernel(scale, starts_ref, *refs):
    *active_refs, dec_ref, out_ref = refs
    rows = active_refs[0].shape[0]
    for index, active_ref in enumerate(active_refs):
        term = lax.dot_general(
            active_ref[...], dec_ref[...], (((1,), (1,)), ((), ())), preferred_element_type=F32
        )
        start = pl.multiple_of(starts_ref[index], rows)
        out_ref[pl.ds(start, rows), :] = (scale * term).astype(out_ref.dtype)


def decode(starts, actives, dec_by_width, scale):
    rows, slab_width = actives[0].shape
    model_width = dec_by_width.shape[0]
    count = len(actives)
    in_vmem = pl.BlockSpec(memory_space=pltpu.VMEM)
    return pl.pallas_call(
        functools.partial(decode_kernel, scale),
        out_shape=jax.ShapeDtypeStruct((count * rows, model_width), BF16),
        in_specs=[pl.BlockSpec(memory_space=pltpu.SMEM)] + [in_vmem] * (count + 1),
        out_specs=in_vmem,
        compiler_params=pltpu.CompilerParams(vmem_limit_bytes=24 * 1024 * 1024),
        cost_estimate=pl.CostEstimate(
            flops=2 * count * rows * slab_width * model_width,
            bytes_accessed=2 * (count * rows + model_width) * slab_width,
            transcendentals=0,
        ),
    )(jnp.stack(starts), *actives, dec_by_width)


def body(layer_acts, enc_weight, dec_weight, enc_bias, dec_bias):
    tok_local = layer_acts[0]
    enc_local = enc_weight[0]
    dec_local = dec_weight[0]
    bias = enc_bias[None, :]
    model_width, slab_width = enc_local.shape
    blocks = lax.axis_size("feat")
    enc_scale = (layer_acts.shape[0] * lax.axis_size("layer") * model_width) ** (-0.5)
    dec_scale = (slab_width * blocks) ** (-0.5)
    tokens = tok_local.shape[0] * blocks
    half, quarter = tokens // 2, tokens // 4
    place = lax.axis_index("layer")
    chip, core = place // 2, place % 2

    def quarter_at(core_index, chip_index):
        return core_index * half + chip_index * quarter

    mine = quarter_at(core, chip)
    of_chip = quarter_at(core, 1 - chip)
    of_core = quarter_at(1 - core, chip)
    of_both = quarter_at(1 - core, 1 - chip)

    whole_tokens = gather_tokens(tok_local)

    def encode(start):
        return dot(rows_of(whole_tokens, start, quarter), enc_local)

    sum_of_chip = encode(of_chip) + to_core(encode(of_both))
    leading = lax.reduce_precision(sum_of_chip, 8, 7)
    remainder = (sum_of_chip - leading).astype(BF16)
    arrived = to_chip(leading.astype(BF16)).astype(F32)
    sum_mine = encode(mine) + to_core(encode(of_core))

    def activate(preact):
        return jnp.maximum(preact, 0.0).astype(BF16)

    active_mine = activate(enc_scale * (sum_mine + arrived) + bias)
    active_of_chip = to_chip(active_mine)
    active_of_core = to_core(active_mine)
    active_of_both = to_core(active_of_chip)
    remainder, active_of_both = lax.optimization_barrier((remainder, active_of_both))

    starts = (mine, of_core, of_chip, of_both)
    actives = (active_mine, active_of_core, active_of_chip, active_of_both)
    recon_terms = decode(starts, actives, dec_local.T, dec_scale)
    arrived_later = to_chip(remainder).astype(F32)
    exact_mine = activate(enc_scale * (sum_mine + (arrived + arrived_later)) + bias)
    arrived_terms = lax.all_to_all(
        recon_terms.reshape(blocks, tokens // blocks, model_width), "feat", 0, 0, tiled=True
    )
    recon = jnp.sum(arrived_terms.astype(F32), axis=0)
    error_b = (recon + dec_bias[0] - tok_local.astype(F32)).astype(BF16)
    error_b, exact_mine = lax.optimization_barrier((error_b, exact_mine))
    exact_of_chip = to_chip(exact_mine)
    whole_errors, exact_of_chip = lax.optimization_barrier((gather_tokens(error_b), exact_of_chip))

    def enc_rows(starts):
        return jnp.concatenate([rows_of(whole_tokens, start, quarter) for start in starts])

    own_rows = (mine, of_chip)
    other_rows = (of_core, of_both)
    errors_other = jnp.concatenate([rows_of(whole_errors, start, quarter) for start in other_rows])
    errors_own = jnp.concatenate([rows_of(whole_errors, start, quarter) for start in own_rows])
    grad_other = dot_transposed(errors_other, dec_local).astype(BF16)
    grad_from_core = to_core(grad_other).astype(F32)
    grad_pair = dot_transposed(errors_own, dec_local) + grad_from_core
    grad_pair_b = grad_pair.astype(BF16)
    from_chip = to_chip(grad_pair_b)
    errors_all = jnp.concatenate([rows_of(whole_errors, start, quarter) for start in starts])
    grad_dec = contract_rows(jnp.concatenate(actives), errors_all)
    dec_step = (-LEARN_RATE * dec_scale * grad_dec).astype(BF16)[None]
    from_chip, dec_step = lax.optimization_barrier((from_chip, dec_step))
    from_chip = from_chip.astype(F32)
    from_chip = jnp.concatenate([from_chip[quarter:], from_chip[:quarter]])
    grad_act = dec_scale * (grad_pair + from_chip)
    exact_own = jnp.concatenate([exact_mine, exact_of_chip])
    grad_pre_own = jnp.where(exact_own > 0, grad_act, 0.0).astype(BF16)
    grad_pre_other = to_core(grad_pre_own)
    grad_enc = contract_rows(enc_rows(own_rows + other_rows), jnp.concatenate([grad_pre_own, grad_pre_other]))
    enc_step = (-LEARN_RATE * enc_scale * grad_enc).astype(BF16)[None]
    return (enc_step, dec_step)


def solution(mesh):
    in_specs = (
        P("layer", "feat", None),
        P("layer", None, "feat"),
        P("layer", "feat", None),
        P("feat"),
        P("layer", None),
    )
    out_specs = (P("layer", None, "feat"), P("layer", "feat", None))
    return jax.shard_map(body, mesh=mesh, in_specs=in_specs, out_specs=out_specs, check_vma=False)
```

```python
import functools

import jax
import jax.numpy as jnp
from jax import lax
from jax.experimental import pallas as pl
from jax.experimental.pallas import tpu as pltpu
from jax.sharding import PartitionSpec as P

LEARN_RATE = 4.0
BF16 = jnp.bfloat16
F32 = jnp.float32
PARTS = 2
STEP_BLOCKS = 1
ACROSS_CORES = [(0, 1), (1, 0), (2, 3), (3, 2)]
ACROSS_CHIPS = [(0, 2), (1, 3), (2, 0), (3, 1)]


def to_core(value):
    return lax.ppermute(value, "layer", ACROSS_CORES)


def to_chip(value):
    return lax.ppermute(value, "layer", ACROSS_CHIPS)


def gather_tokens(value):
    blocks = lax.axis_size("feat")
    rows, width = value.shape
    copies = jnp.broadcast_to(value[None], (blocks, rows, width))
    return lax.all_to_all(copies, "feat", 0, 0, tiled=True).reshape(blocks * rows, width)


def rows_of(value, start, count):
    return lax.dynamic_slice_in_dim(value, start, count, axis=0)


def dot(left, right):
    return jnp.dot(left, right, preferred_element_type=F32)


def dot_transposed(left, right):
    return lax.dot_general(left, right, (((1,), (1,)), ((), ())), preferred_element_type=F32)


def contract_rows(left, right):
    return lax.dot_general(left, right, (((0,), (0,)), ((), ())), preferred_element_type=F32)


VMEM = pl.BlockSpec(memory_space=pltpu.VMEM)
SMEM = pl.BlockSpec(memory_space=pltpu.SMEM)


def local_call(kernel, out_shape, operands, flops):
    moved = sum(operand.size * operand.dtype.itemsize for operand in operands)
    return pl.pallas_call(
        kernel,
        out_shape=out_shape,
        in_specs=[SMEM] + [VMEM] * (len(operands) - 1),
        out_specs=jax.tree.map(lambda _: VMEM, out_shape),
        compiler_params=pltpu.CompilerParams(vmem_limit_bytes=24 * 1024 * 1024),
        cost_estimate=pl.CostEstimate(flops=flops, bytes_accessed=moved, transcendentals=0),
    )(*operands)


def decode_kernel(places, part_count, has_before, scale, starts_ref, *refs):
    piece_refs = refs[: len(places)]
    dec_refs = refs[len(places) : len(places) + part_count]
    before_ref = refs[-2] if has_before else None
    out_ref = refs[-1]
    rows = piece_refs[0].shape[0]
    for row in range(out_ref.shape[0] // rows):
        where = pl.ds(pl.multiple_of(starts_ref[row], rows), rows)
        total = before_ref[where, :] if has_before else None
        for (row_of_piece, part), piece_ref in zip(places, piece_refs):
            if row_of_piece == row:
                term = dot_transposed(piece_ref[...], dec_refs[part][...])
                total = term if total is None else total + term
        out_ref[where, :] = (scale * total).astype(out_ref.dtype)


def decode(starts, pieces, dec_parts, before, scale, dtype):
    places, arrays = list(pieces), list(pieces.values())
    rows, part_width = arrays[0].shape
    model_width = dec_parts[0].shape[0]
    operands = [starts, *arrays, *dec_parts] + ([] if before is None else [before])
    kernel = functools.partial(decode_kernel, places, len(dec_parts), before is not None, scale)
    out_shape = jax.ShapeDtypeStruct((starts.shape[0] * rows, model_width), dtype)
    return local_call(kernel, out_shape, operands, 2 * len(places) * rows * part_width * model_width)


def back_kernel(row, rows, part_count, has_terms, starts_ref, errors_ref, *refs):
    dec_refs, refs = refs[:part_count], refs[part_count:]
    term_refs, out_refs = (refs[:part_count], refs[part_count:]) if has_terms else (None, refs)
    errors = errors_ref[pl.ds(pl.multiple_of(starts_ref[row], rows), rows), :]
    for part in range(part_count):
        total = dot(errors, dec_refs[part][...])
        if has_terms:
            total += term_refs[part][...].astype(F32)
        out_refs[part][...] = total.astype(out_refs[part].dtype)


def back(starts, row, errors, dec_parts, terms, dtype):
    rows = errors.shape[0] // starts.shape[0]
    model_width, part_width = dec_parts[0].shape
    operands = [starts, errors, *dec_parts] + ([] if terms is None else terms)
    kernel = functools.partial(back_kernel, row, rows, len(dec_parts), terms is not None)
    out_shape = [jax.ShapeDtypeStruct((rows, part_width), dtype)] * len(dec_parts)
    return local_call(kernel, out_shape, operands, 2 * rows * part_width * model_width * len(dec_parts))


def step_kernel(scale, left_ref, *refs):
    *piece_refs, _, out_ref = refs
    rows = jnp.concatenate([piece_ref[...] for piece_ref in piece_refs], axis=0)
    out_ref[...] = (scale * contract_rows(left_ref[...], rows)).astype(out_ref.dtype)


def first_step_kernel(scale, *refs):
    step_kernel(scale, *refs[:-1], None, refs[-1])


def write_step(left, pieces, before, part_index, scale):
    rows, part_width = pieces[0].shape
    tokens, model_width = left.shape
    block = part_width // STEP_BLOCKS
    operands = [left, *pieces]
    in_specs = [pl.BlockSpec((tokens, model_width), lambda index: (0, 0))]
    in_specs += [pl.BlockSpec((rows, block), lambda index: (0, index))] * len(pieces)
    kernel, aliases = first_step_kernel, {}
    if before is not None:
        aliases = {len(operands): 0}
        operands.append(before)
        in_specs.append(pl.BlockSpec(memory_space=pl.ANY))
        kernel = step_kernel
    first_block = part_index * STEP_BLOCKS
    return pl.pallas_call(
        functools.partial(kernel, scale),
        grid=(STEP_BLOCKS,),
        out_shape=jax.ShapeDtypeStruct((model_width, part_width * PARTS), BF16),
        in_specs=in_specs,
        out_specs=pl.BlockSpec((model_width, block), lambda index: (0, first_block + index)),
        input_output_aliases=aliases,
        compiler_params=pltpu.CompilerParams(vmem_limit_bytes=16 * 1024 * 1024),
        cost_estimate=pl.CostEstimate(
            flops=2 * tokens * part_width * model_width,
            bytes_accessed=2 * (tokens + model_width) * part_width,
            transcendentals=0,
        ),
    )(*operands)


def body(layer_acts, enc_weight, dec_weight, enc_bias, dec_bias):
    tok_local = layer_acts[0]
    enc_local = enc_weight[0]
    dec_local = dec_weight[0]
    bias = enc_bias[None, :]
    model_width, slab_width = enc_local.shape
    blocks = lax.axis_size("feat")
    enc_scale = (layer_acts.shape[0] * lax.axis_size("layer") * model_width) ** (-0.5)
    dec_scale = (slab_width * blocks) ** (-0.5)
    tokens = tok_local.shape[0] * blocks
    half, quarter = tokens // 2, tokens // 4
    place = lax.axis_index("layer")
    chip, core = place // 2, place % 2

    def quarter_at(core_index, chip_index):
        return core_index * half + chip_index * quarter

    mine = quarter_at(core, chip)
    of_chip = quarter_at(core, 1 - chip)
    of_core = quarter_at(1 - core, chip)
    of_both = quarter_at(1 - core, 1 - chip)
    starts = (mine, of_core, of_chip, of_both)
    starts_array = jnp.stack(starts)

    whole_tokens = gather_tokens(tok_local)
    token_rows = [rows_of(whole_tokens, start, quarter) for start in starts]
    tok_mine, tok_of_core, tok_of_chip, tok_of_both = token_rows

    def activate(sums, part):
        return jnp.maximum(enc_scale * sums + bias[:, part], 0.0).astype(BF16)

    part_width = slab_width // PARTS
    parts = [slice(index * part_width, (index + 1) * part_width) for index in range(PARTS)]
    remainders, sums_mine, arrived, actives = [], [], [], []
    for part in parts:
        enc_part = enc_local[:, part]
        sum_of_chip = dot(tok_of_chip, enc_part) + to_core(dot(tok_of_both, enc_part))
        leading = lax.reduce_precision(sum_of_chip, 8, 7)
        remainders.append((sum_of_chip - leading).astype(BF16))
        arrived.append(to_chip(leading.astype(BF16)))
        sums_mine.append(dot(tok_mine, enc_part) + to_core(dot(tok_of_core, enc_part)))
    dec_parts = [dec_local.T[:, part] for part in parts]
    active = {}
    for index, part in enumerate(parts):
        active[0, index] = activate(sums_mine[index] + arrived[index].astype(F32), part)
        active[1, index] = to_core(active[0, index])
        active[2, index] = to_chip(active[0, index])
    last = PARTS - 1
    for index in range(last):
        active[3, index] = to_core(active[2, index])
    early = {place: value for place, value in active.items() if place != (2, last)}
    recon_early = decode(starts_array, early, dec_parts, None, 1.0, F32)
    active[2, last], recon_early = lax.optimization_barrier((active[2, last], recon_early))
    active[3, last] = to_core(active[2, last])
    late = {(2, last): active[2, last], (3, last): active[3, last]}
    recon_terms = decode(starts_array, late, dec_parts, recon_early, dec_scale, BF16)
    remainders, recon_terms = lax.optimization_barrier((remainders, recon_terms))
    arrived_later = [to_chip(remainder) for remainder in remainders]
    arrived_terms = lax.all_to_all(
        recon_terms.reshape(blocks, tokens // blocks, model_width), "feat", 0, 0, tiled=True
    )
    recon = jnp.sum(arrived_terms.astype(F32), axis=0)
    error_b = (recon + dec_bias[0] - tok_local.astype(F32)).astype(BF16)
    error_b, arrived_later[0] = lax.optimization_barrier((error_b, arrived_later[0]))
    whole_errors, arrived_later = lax.optimization_barrier((gather_tokens(error_b), arrived_later))
    of_both_b = back(starts_array, 3, whole_errors, dec_parts, None, BF16)
    whole_errors, of_both_b = lax.optimization_barrier((whole_errors, of_both_b))
    of_core_b = back(starts_array, 1, whole_errors, dec_parts, None, BF16)
    pair_b = back(starts_array, 2, whole_errors, dec_parts, [to_core(term) for term in of_both_b], BF16)
    whole_errors, pair_b = lax.optimization_barrier((whole_errors, pair_b))
    grads_arrived = [to_chip(term) for term in pair_b]
    grads_mine = back(starts_array, 0, whole_errors, dec_parts, [to_core(term) for term in of_core_b], F32)

    whole_errors, arrived_later, grads_mine = lax.optimization_barrier((whole_errors, arrived_later, grads_mine))
    alive = []
    for index, part in enumerate(parts):
        terms = arrived[index].astype(F32) + arrived_later[index].astype(F32)
        exact = enc_scale * (sums_mine[index] + terms) + bias[:, part]
        alive.append((exact > 0.0).astype(F32))
    errors = jnp.concatenate([rows_of(whole_errors, start, quarter) for start in starts])
    dec_step = enc_step = None
    for index in range(PARTS):
        pieces = [active[row, index] for row in range(4)]
        dec_step = write_step(errors, pieces, dec_step, index, -LEARN_RATE * dec_scale)
    grads_arrived[0], dec_step, alive = lax.optimization_barrier((grads_arrived[0], dec_step, alive))

    pres = []
    for index in range(PARTS):
        grad_arrived = grads_arrived[index]
        if index:
            grad_arrived, pres[-1][1] = lax.optimization_barrier((grad_arrived, pres[-1][1]))
        grad_act = dec_scale * (grads_mine[index] + grad_arrived.astype(F32))
        pre_mine = jnp.where(alive[index] > 0.0, grad_act, 0.0).astype(BF16)
        pres.append([pre_mine, to_core(pre_mine), to_chip(pre_mine)])
        if index:
            pres[0][2], pres[1][2] = lax.optimization_barrier((pres[0][2], pres[1][2]))
    all_tokens = jnp.concatenate(token_rows)
    for index in range(PARTS):
        pre_mine, pre_of_core, pre_of_chip = pres[index]
        pieces = [pre_mine, pre_of_core, pre_of_chip, to_core(pre_of_chip)]
        enc_step = write_step(all_tokens, pieces, enc_step, index, -LEARN_RATE * enc_scale)
    return (enc_step[None], dec_step.T[None])


def solution(mesh):
    in_specs = (
        P("layer", "feat", None),
        P("layer", None, "feat"),
        P("layer", "feat", None),
        P("feat"),
        P("layer", None),
    )
    out_specs = (P("layer", None, "feat"), P("layer", "feat", None))
    return jax.shard_map(body, mesh=mesh, in_specs=in_specs, out_specs=out_specs, check_vma=False)
```

```python
import functools

import jax
import jax.numpy as jnp
from jax import lax
from jax.experimental import pallas as pl
from jax.experimental.pallas import tpu as pltpu
from jax.sharding import PartitionSpec as P

LEARN_RATE = 4.0
BF16 = jnp.bfloat16
F32 = jnp.float32
PARTS = 2
ACROSS_CORES = [(0, 1), (1, 0), (2, 3), (3, 2)]
ACROSS_CHIPS = [(0, 2), (1, 3), (2, 0), (3, 1)]


def to_core(value):
    return lax.ppermute(value, "layer", ACROSS_CORES)


def to_chip(value):
    return lax.ppermute(value, "layer", ACROSS_CHIPS)


def gather_tokens(value):
    blocks = lax.axis_size("feat")
    rows, width = value.shape
    copies = jnp.broadcast_to(value[None], (blocks, rows, width))
    return lax.all_to_all(copies, "feat", 0, 0, tiled=True).reshape(blocks * rows, width)


def rows_of(value, start, count):
    return lax.dynamic_slice_in_dim(value, start, count, axis=0)


def dot(left, right):
    return jnp.dot(left, right, preferred_element_type=F32)


def dot_transposed(left, right):
    return lax.dot_general(left, right, (((1,), (1,)), ((), ())), preferred_element_type=F32)


def contract_rows(left, right):
    return lax.dot_general(left, right, (((0,), (0,)), ((), ())), preferred_element_type=F32)


VMEM = pl.BlockSpec(memory_space=pltpu.VMEM)
SMEM = pl.BlockSpec(memory_space=pltpu.SMEM)


def local_call(kernel, out_shape, operands, flops):
    moved = sum(operand.size * operand.dtype.itemsize for operand in operands)
    return pl.pallas_call(
        kernel,
        out_shape=out_shape,
        in_specs=[SMEM] + [VMEM] * (len(operands) - 1),
        out_specs=jax.tree.map(lambda _: VMEM, out_shape),
        compiler_params=pltpu.CompilerParams(vmem_limit_bytes=24 * 1024 * 1024),
        cost_estimate=pl.CostEstimate(flops=flops, bytes_accessed=moved, transcendentals=0),
    )(*operands)


def decode_kernel(places, part_count, has_before, scale, starts_ref, *refs):
    piece_refs = refs[: len(places)]
    dec_refs = refs[len(places) : len(places) + part_count]
    before_ref = refs[-2] if has_before else None
    out_ref = refs[-1]
    rows = piece_refs[0].shape[0]
    terms = {}
    for part in range(part_count):
        owners = [row for row, part_of_piece in places if part_of_piece == part]
        pieces = [ref[...] for (_, part_of_piece), ref in zip(places, piece_refs) if part_of_piece == part]
        if not pieces:
            continue
        product = dot_transposed(jnp.concatenate(pieces, axis=0), dec_refs[part][...])
        for index, row in enumerate(owners):
            terms.setdefault(row, []).append(product[index * rows : (index + 1) * rows])
    for row in range(out_ref.shape[0] // rows):
        where = pl.ds(pl.multiple_of(starts_ref[row], rows), rows)
        summands = terms.get(row, []) + ([before_ref[where, :]] if has_before else [])
        out_ref[where, :] = (scale * sum(summands[1:], summands[0])).astype(out_ref.dtype)


def decode(starts, pieces, dec_parts, before, scale, dtype):
    places, arrays = list(pieces), list(pieces.values())
    rows, part_width = arrays[0].shape
    model_width = dec_parts[0].shape[0]
    operands = [starts, *arrays, *dec_parts] + ([] if before is None else [before])
    kernel = functools.partial(decode_kernel, places, len(dec_parts), before is not None, scale)
    out_shape = jax.ShapeDtypeStruct((starts.shape[0] * rows, model_width), dtype)
    return local_call(kernel, out_shape, operands, 2 * len(places) * rows * part_width * model_width)


def back_kernel(row, rows, part_count, has_terms, starts_ref, errors_ref, *refs):
    dec_refs, refs = refs[:part_count], refs[part_count:]
    term_refs, out_refs = (refs[:part_count], refs[part_count:]) if has_terms else (None, refs)
    errors = errors_ref[pl.ds(pl.multiple_of(starts_ref[row], rows), rows), :]
    for part in range(part_count):
        total = dot(errors, dec_refs[part][...])
        if has_terms:
            total += term_refs[part][...].astype(F32)
        out_refs[part][...] = total.astype(out_refs[part].dtype)


def back(starts, row, errors, dec_parts, terms, dtype):
    rows = errors.shape[0] // starts.shape[0]
    model_width, part_width = dec_parts[0].shape
    operands = [starts, errors, *dec_parts] + ([] if terms is None else terms)
    kernel = functools.partial(back_kernel, row, rows, len(dec_parts), terms is not None)
    out_shape = [jax.ShapeDtypeStruct((rows, part_width), dtype)] * len(dec_parts)
    return local_call(kernel, out_shape, operands, 2 * rows * part_width * model_width * len(dec_parts))


def step_kernel(scale, part_count, piece_count, left_ref, *refs):
    out_ref = refs[-1]
    for part in range(part_count):

        @pl.when(pl.program_id(0) == part)
        def _(part=part):
            pieces = [ref[...] for ref in refs[piece_count * part : piece_count * (part + 1)]]
            total = contract_rows(left_ref[...], jnp.concatenate(pieces, axis=0))
            out_ref[...] = (scale * total).astype(out_ref.dtype)


def write_step(left, pieces, scale):
    part_count, piece_count = len(pieces), len(pieces[0])
    part_width = pieces[0][0].shape[1]
    model_width = left.shape[1]
    operands = [left, *(piece for part in pieces for piece in part)]
    return pl.pallas_call(
        functools.partial(step_kernel, scale, part_count, piece_count),
        grid=(part_count,),
        out_shape=jax.ShapeDtypeStruct((model_width, part_width * part_count), BF16),
        in_specs=[VMEM] * len(operands),
        out_specs=pl.BlockSpec((model_width, part_width), lambda index: (0, index)),
        compiler_params=pltpu.CompilerParams(vmem_limit_bytes=24 * 1024 * 1024),
        cost_estimate=pl.CostEstimate(
            flops=2 * left.size * part_width * part_count,
            bytes_accessed=2 * (left.shape[0] + model_width) * part_width * part_count,
            transcendentals=0,
        ),
    )(*operands)


def body(layer_acts, enc_weight, dec_weight, enc_bias, dec_bias):
    tok_local = layer_acts[0]
    enc_local = enc_weight[0]
    dec_local = dec_weight[0]
    bias = enc_bias[None, :]
    model_width, slab_width = enc_local.shape
    blocks = lax.axis_size("feat")
    enc_scale = (layer_acts.shape[0] * lax.axis_size("layer") * model_width) ** (-0.5)
    dec_scale = (slab_width * blocks) ** (-0.5)
    tokens = tok_local.shape[0] * blocks
    half, quarter = tokens // 2, tokens // 4
    place = lax.axis_index("layer")
    chip, core = place // 2, place % 2

    def quarter_at(core_index, chip_index):
        return core_index * half + chip_index * quarter

    mine = quarter_at(core, chip)
    of_chip = quarter_at(core, 1 - chip)
    of_core = quarter_at(1 - core, chip)
    of_both = quarter_at(1 - core, 1 - chip)
    starts = (mine, of_core, of_chip, of_both)
    starts_array = jnp.stack(starts)

    whole_tokens = gather_tokens(tok_local)
    token_rows = [rows_of(whole_tokens, start, quarter) for start in starts]
    tok_mine, tok_of_core, tok_of_chip, tok_of_both = token_rows

    def activate(sums, part):
        return jnp.maximum(enc_scale * sums + bias[:, part], 0.0).astype(BF16)

    part_width = slab_width // PARTS
    parts = [slice(index * part_width, (index + 1) * part_width) for index in range(PARTS)]
    remainders, leading_b, sums_mine = [], [], []
    for part in parts:
        enc_part = enc_local[:, part]
        sum_of_chip = dot(tok_of_chip, enc_part) + to_core(dot(tok_of_both, enc_part))
        leading = lax.reduce_precision(sum_of_chip, 8, 7)
        remainders.append((sum_of_chip - leading).astype(BF16))
        leading_b.append(leading.astype(BF16))
    arrived = [to_chip(piece) for piece in leading_b]
    ties = [leading_b[0]] * PARTS
    for index, part in enumerate(parts):
        enc_part = enc_local[:, part]
        near, cross, _ = lax.optimization_barrier((tok_mine, tok_of_core, ties[index]))
        sums_mine.append(dot(near, enc_part) + to_core(dot(cross, enc_part)))
    dec_parts = [dec_local.T[:, part] for part in parts]
    active = {}
    for index, part in enumerate(parts):
        active[0, index] = activate(sums_mine[index] + arrived[index].astype(F32), part)
        active[1, index] = to_core(active[0, index])
        active[2, index] = to_chip(active[0, index])
    last = PARTS - 1
    for index in range(last):
        active[3, index] = to_core(active[2, index])
    early = {place: value for place, value in active.items() if place != (2, last)}
    recon_early = decode(starts_array, early, dec_parts, None, 1.0, F32)
    active[2, last], recon_early = lax.optimization_barrier((active[2, last], recon_early))
    active[3, last] = to_core(active[2, last])
    late = {(2, last): active[2, last], (3, last): active[3, last]}
    recon_terms = decode(starts_array, late, dec_parts, recon_early, dec_scale, BF16)
    remainders, recon_terms = lax.optimization_barrier((remainders, recon_terms))
    arrived_later = [to_chip(remainder) for remainder in remainders]
    arrived_terms = lax.all_to_all(
        recon_terms.reshape(blocks, tokens // blocks, model_width), "feat", 0, 0, tiled=True
    )
    recon = jnp.sum(arrived_terms.astype(F32), axis=0)
    error_b = (recon + dec_bias[0] - tok_local.astype(F32)).astype(BF16)
    error_b, arrived_later[0] = lax.optimization_barrier((error_b, arrived_later[0]))
    whole_errors, arrived_later = lax.optimization_barrier((gather_tokens(error_b), arrived_later))
    of_both_b = back(starts_array, 3, whole_errors, dec_parts, None, BF16)
    whole_errors, of_both_b = lax.optimization_barrier((whole_errors, of_both_b))
    of_core_b = back(starts_array, 1, whole_errors, dec_parts, None, BF16)
    pair_b = back(starts_array, 2, whole_errors, dec_parts, [to_core(term) for term in of_both_b], BF16)
    whole_errors, pair_b = lax.optimization_barrier((whole_errors, pair_b))
    grads_arrived = [to_chip(term) for term in pair_b]
    grads_mine = back(starts_array, 0, whole_errors, dec_parts, [to_core(term) for term in of_core_b], F32)

    whole_errors, arrived_later, grads_mine = lax.optimization_barrier((whole_errors, arrived_later, grads_mine))
    alive = []
    for index, part in enumerate(parts):
        terms = arrived[index].astype(F32) + arrived_later[index].astype(F32)
        exact = enc_scale * (sums_mine[index] + terms) + bias[:, part]
        alive.append((exact > 0.0).astype(F32))
    errors = jnp.concatenate([rows_of(whole_errors, start, quarter) for start in starts])
    pieces = [[active[row, index] for row in range(4)] for index in range(PARTS)]
    dec_step = write_step(errors, pieces, -LEARN_RATE * dec_scale)
    grads_arrived[0], dec_step, alive = lax.optimization_barrier((grads_arrived[0], dec_step, alive))

    pres_mine, pres_of_core, pres_of_chip = [], [], []
    for index in range(PARTS):
        grad_arrived = grads_arrived[index]
        if index:
            grad_arrived, pres_of_core[-1] = lax.optimization_barrier((grad_arrived, pres_of_core[-1]))
        grad_act = dec_scale * (grads_mine[index] + grad_arrived.astype(F32))
        pre_mine = jnp.where(alive[index] > 0.0, grad_act, 0.0).astype(BF16)
        pres_mine.append(pre_mine)
        pres_of_core.append(to_core(pre_mine))
        pres_of_chip.append(to_chip(pre_mine))
    pres_of_chip = lax.optimization_barrier(pres_of_chip)
    pieces = [
        [mine, near, far, to_core(far)] for mine, near, far in zip(pres_mine, pres_of_core, pres_of_chip)
    ]
    enc_step = write_step(jnp.concatenate(token_rows), pieces, -LEARN_RATE * enc_scale)
    return (enc_step[None], dec_step.T[None])


def solution(mesh):
    in_specs = (
        P("layer", "feat", None),
        P("layer", None, "feat"),
        P("layer", "feat", None),
        P("feat"),
        P("layer", None),
    )
    out_specs = (P("layer", None, "feat"), P("layer", "feat", None))
    return jax.shard_map(body, mesh=mesh, in_specs=in_specs, out_specs=out_specs, check_vma=False)
```

```python
import functools

import jax
import jax.numpy as jnp
from jax import lax
from jax.experimental import pallas as pl
from jax.experimental.pallas import tpu as pltpu
from jax.sharding import PartitionSpec as P

LEARN_RATE = 4.0
BF16 = jnp.bfloat16
F32 = jnp.float32
PARTS = 2
ACROSS_CORES = [(0, 1), (1, 0), (2, 3), (3, 2)]
ACROSS_CHIPS = [(0, 2), (1, 3), (2, 0), (3, 1)]


def to_core(value):
    return lax.ppermute(value, "layer", ACROSS_CORES)


def to_chip(value):
    return lax.ppermute(value, "layer", ACROSS_CHIPS)


def gather_tokens(value):
    blocks = lax.axis_size("feat")
    rows, width = value.shape
    copies = jnp.broadcast_to(value[None], (blocks, rows, width))
    return lax.all_to_all(copies, "feat", 0, 0, tiled=True).reshape(blocks * rows, width)


def rows_of(value, start, count):
    return lax.dynamic_slice_in_dim(value, start, count, axis=0)


def dot(left, right):
    return jnp.dot(left, right, preferred_element_type=F32)


def dot_transposed(left, right):
    return lax.dot_general(left, right, (((1,), (1,)), ((), ())), preferred_element_type=F32)


def contract_rows(left, right):
    return lax.dot_general(left, right, (((0,), (0,)), ((), ())), preferred_element_type=F32)


VMEM = pl.BlockSpec(memory_space=pltpu.VMEM)
SMEM = pl.BlockSpec(memory_space=pltpu.SMEM)


def local_call(kernel, out_shape, operands, flops):
    moved = sum(operand.size * operand.dtype.itemsize for operand in operands)
    return pl.pallas_call(
        kernel,
        out_shape=out_shape,
        in_specs=[SMEM] + [VMEM] * (len(operands) - 1),
        out_specs=jax.tree.map(lambda _: VMEM, out_shape),
        compiler_params=pltpu.CompilerParams(vmem_limit_bytes=24 * 1024 * 1024),
        cost_estimate=pl.CostEstimate(flops=flops, bytes_accessed=moved, transcendentals=0),
    )(*operands)


def decode_kernel(places, part_count, has_before, scale, starts_ref, *refs):
    piece_refs = refs[: len(places)]
    dec_refs = refs[len(places) : len(places) + part_count]
    before_ref = refs[-2] if has_before else None
    out_ref = refs[-1]
    rows = piece_refs[0].shape[0]
    terms = {}
    for part in range(part_count):
        owners = [row for row, part_of_piece in places if part_of_piece == part]
        pieces = [ref[...] for (_, part_of_piece), ref in zip(places, piece_refs) if part_of_piece == part]
        if not pieces:
            continue
        product = dot_transposed(jnp.concatenate(pieces, axis=0), dec_refs[part][...])
        for index, row in enumerate(owners):
            terms.setdefault(row, []).append(product[index * rows : (index + 1) * rows])
    for row in range(out_ref.shape[0] // rows):
        where = pl.ds(pl.multiple_of(starts_ref[row], rows), rows)
        summands = terms.get(row, []) + ([before_ref[where, :]] if has_before else [])
        out_ref[where, :] = (scale * sum(summands[1:], summands[0])).astype(out_ref.dtype)


def decode(starts, pieces, dec_parts, before, scale, dtype):
    places, arrays = list(pieces), list(pieces.values())
    rows, part_width = arrays[0].shape
    model_width = dec_parts[0].shape[0]
    operands = [starts, *arrays, *dec_parts] + ([] if before is None else [before])
    kernel = functools.partial(decode_kernel, places, len(dec_parts), before is not None, scale)
    out_shape = jax.ShapeDtypeStruct((starts.shape[0] * rows, model_width), dtype)
    return local_call(kernel, out_shape, operands, 2 * len(places) * rows * part_width * model_width)


def back_kernel(row, rows, part_count, has_terms, starts_ref, errors_ref, *refs):
    dec_refs, refs = refs[:part_count], refs[part_count:]
    term_refs, out_refs = (refs[:part_count], refs[part_count:]) if has_terms else (None, refs)
    errors = errors_ref[pl.ds(pl.multiple_of(starts_ref[row], rows), rows), :]
    for part in range(part_count):
        total = dot(errors, dec_refs[part][...])
        if has_terms:
            total += term_refs[part][...].astype(F32)
        out_refs[part][...] = total.astype(out_refs[part].dtype)


def back_rows_kernel(rows_of_outputs, rows, part_count, starts_ref, errors_ref, *refs):
    dec_refs, out_refs = refs[:part_count], refs[part_count:]
    errors = [errors_ref[pl.ds(pl.multiple_of(starts_ref[row], rows), rows), :] for row in rows_of_outputs]
    errors = jnp.concatenate(errors, axis=0)
    for part in range(part_count):
        total = dot(errors, dec_refs[part][...])
        for index in range(len(rows_of_outputs)):
            out_ref = out_refs[index * part_count + part]
            out_ref[...] = total[index * rows : (index + 1) * rows].astype(out_ref.dtype)


def back_rows(starts, rows_of_outputs, errors, dec_parts):
    rows, count = errors.shape[0] // starts.shape[0], len(dec_parts)
    model_width, part_width = dec_parts[0].shape
    kernel = functools.partial(back_rows_kernel, rows_of_outputs, rows, count)
    out_shape = [jax.ShapeDtypeStruct((rows, part_width), BF16)] * (count * len(rows_of_outputs))
    flops = 2 * rows * part_width * model_width * len(out_shape)
    outs = local_call(kernel, out_shape, [starts, errors, *dec_parts], flops)
    return [outs[index * count : (index + 1) * count] for index in range(len(rows_of_outputs))]


def back(starts, row, errors, dec_parts, terms, dtype):
    rows = errors.shape[0] // starts.shape[0]
    model_width, part_width = dec_parts[0].shape
    operands = [starts, errors, *dec_parts] + ([] if terms is None else terms)
    kernel = functools.partial(back_kernel, row, rows, len(dec_parts), terms is not None)
    out_shape = [jax.ShapeDtypeStruct((rows, part_width), dtype)] * len(dec_parts)
    return local_call(kernel, out_shape, operands, 2 * rows * part_width * model_width * len(dec_parts))


def step_kernel(scale, part_count, piece_count, left_ref, *refs):
    out_ref = refs[-1]
    for part in range(part_count):

        @pl.when(pl.program_id(0) == part)
        def _(part=part):
            pieces = [ref[...] for ref in refs[piece_count * part : piece_count * (part + 1)]]
            total = contract_rows(left_ref[...], jnp.concatenate(pieces, axis=0))
            out_ref[...] = (scale * total).astype(out_ref.dtype)


def write_step(left, pieces, scale):
    part_count, piece_count = len(pieces), len(pieces[0])
    part_width = pieces[0][0].shape[1]
    model_width = left.shape[1]
    operands = [left, *(piece for part in pieces for piece in part)]
    return pl.pallas_call(
        functools.partial(step_kernel, scale, part_count, piece_count),
        grid=(part_count,),
        out_shape=jax.ShapeDtypeStruct((model_width, part_width * part_count), BF16),
        in_specs=[VMEM] * len(operands),
        out_specs=pl.BlockSpec((model_width, part_width), lambda index: (0, index)),
        compiler_params=pltpu.CompilerParams(vmem_limit_bytes=24 * 1024 * 1024),
        cost_estimate=pl.CostEstimate(
            flops=2 * left.size * part_width * part_count,
            bytes_accessed=2 * (left.shape[0] + model_width) * part_width * part_count,
            transcendentals=0,
        ),
    )(*operands)


def body(layer_acts, enc_weight, dec_weight, enc_bias, dec_bias):
    tok_local = layer_acts[0]
    enc_local = enc_weight[0]
    dec_local = dec_weight[0]
    bias = enc_bias[None, :]
    model_width, slab_width = enc_local.shape
    blocks = lax.axis_size("feat")
    enc_scale = (layer_acts.shape[0] * lax.axis_size("layer") * model_width) ** (-0.5)
    dec_scale = (slab_width * blocks) ** (-0.5)
    tokens = tok_local.shape[0] * blocks
    half, quarter = tokens // 2, tokens // 4
    place = lax.axis_index("layer")
    chip, core = place // 2, place % 2

    def quarter_at(core_index, chip_index):
        return core_index * half + chip_index * quarter

    mine = quarter_at(core, chip)
    of_chip = quarter_at(core, 1 - chip)
    of_core = quarter_at(1 - core, chip)
    of_both = quarter_at(1 - core, 1 - chip)
    starts = (mine, of_core, of_chip, of_both)
    starts_array = jnp.stack(starts)

    whole_tokens = gather_tokens(tok_local)
    token_rows = [rows_of(whole_tokens, start, quarter) for start in starts]
    tok_mine, tok_of_core, tok_of_chip, tok_of_both = token_rows

    def activate(sums, part):
        return jnp.maximum(enc_scale * sums + bias[:, part], 0.0).astype(BF16)

    part_width = slab_width // PARTS
    parts = [slice(index * part_width, (index + 1) * part_width) for index in range(PARTS)]
    remainders, leading_b, sums_mine = [], [], []
    for part in parts:
        enc_part = enc_local[:, part]
        sum_of_chip = dot(tok_of_chip, enc_part) + to_core(dot(tok_of_both, enc_part))
        leading = lax.reduce_precision(sum_of_chip, 8, 7)
        remainders.append((sum_of_chip - leading).astype(BF16))
        leading_b.append(leading.astype(BF16))
    arrived = [to_chip(piece) for piece in leading_b]
    ties = [leading_b[0]] * PARTS
    for index, part in enumerate(parts):
        enc_part = enc_local[:, part]
        near, cross, _ = lax.optimization_barrier((tok_mine, tok_of_core, ties[index]))
        sums_mine.append(dot(near, enc_part) + to_core(dot(cross, enc_part)))
    dec_parts = [dec_local.T[:, part] for part in parts]
    active = {}
    for index, part in enumerate(parts):
        active[0, index] = activate(sums_mine[index] + arrived[index].astype(F32), part)
        active[1, index] = to_core(active[0, index])
        active[2, index] = to_chip(active[0, index])
    last = PARTS - 1
    for index in range(last):
        active[3, index] = to_core(active[2, index])
    early = {place: value for place, value in active.items() if place != (2, last)}
    recon_early = decode(starts_array, early, dec_parts, None, 1.0, F32)
    active[2, last], recon_early = lax.optimization_barrier((active[2, last], recon_early))
    active[3, last] = to_core(active[2, last])
    late = {(2, last): active[2, last], (3, last): active[3, last]}
    recon_terms = decode(starts_array, late, dec_parts, recon_early, dec_scale, BF16)
    remainders, recon_terms = lax.optimization_barrier((remainders, recon_terms))
    arrived_later = [to_chip(remainder) for remainder in remainders]
    arrived_terms = lax.all_to_all(
        recon_terms.reshape(blocks, tokens // blocks, model_width), "feat", 0, 0, tiled=True
    )
    recon = jnp.sum(arrived_terms.astype(F32), axis=0)
    error_b = (recon + dec_bias[0] - tok_local.astype(F32)).astype(BF16)
    error_b, arrived_later[0] = lax.optimization_barrier((error_b, arrived_later[0]))
    whole_errors, arrived_later = lax.optimization_barrier((gather_tokens(error_b), arrived_later))
    of_both_b, of_core_b = back_rows(starts_array, (3, 1), whole_errors, dec_parts)
    pair_b = back(starts_array, 2, whole_errors, dec_parts, [to_core(term) for term in of_both_b], BF16)
    whole_errors, pair_b = lax.optimization_barrier((whole_errors, pair_b))
    grads_arrived = [to_chip(term) for term in pair_b]
    grads_mine = back(starts_array, 0, whole_errors, dec_parts, [to_core(term) for term in of_core_b], F32)

    whole_errors, arrived_later, grads_mine = lax.optimization_barrier((whole_errors, arrived_later, grads_mine))
    alive = []
    for index, part in enumerate(parts):
        terms = arrived[index].astype(F32) + arrived_later[index].astype(F32)
        exact = enc_scale * (sums_mine[index] + terms) + bias[:, part]
        alive.append((exact > 0.0).astype(F32))
    errors = jnp.concatenate([rows_of(whole_errors, start, quarter) for start in starts])
    pieces = [[active[row, index] for row in range(4)] for index in range(PARTS)]
    dec_step = write_step(errors, pieces, -LEARN_RATE * dec_scale)
    grads_arrived[0], dec_step, alive = lax.optimization_barrier((grads_arrived[0], dec_step, alive))

    pres_mine, pres_of_core, pres_of_chip = [], [], []
    for index in range(PARTS):
        grad_arrived = grads_arrived[index]
        if index:
            grad_arrived, pres_of_core[-1] = lax.optimization_barrier((grad_arrived, pres_of_core[-1]))
        grad_act = dec_scale * (grads_mine[index] + grad_arrived.astype(F32))
        pre_mine = jnp.where(alive[index] > 0.0, grad_act, 0.0).astype(BF16)
        pres_mine.append(pre_mine)
        pres_of_core.append(to_core(pre_mine))
        pres_of_chip.append(to_chip(pre_mine))
    pres_of_chip = lax.optimization_barrier(pres_of_chip)
    pieces = [
        [mine, near, far, to_core(far)] for mine, near, far in zip(pres_mine, pres_of_core, pres_of_chip)
    ]
    enc_step = write_step(jnp.concatenate(token_rows), pieces, -LEARN_RATE * enc_scale)
    return (enc_step[None], dec_step.T[None])


def solution(mesh):
    in_specs = (
        P("layer", "feat", None),
        P("layer", None, "feat"),
        P("layer", "feat", None),
        P("feat"),
        P("layer", None),
    )
    out_specs = (P("layer", None, "feat"), P("layer", "feat", None))
    return jax.shard_map(body, mesh=mesh, in_specs=in_specs, out_specs=out_specs, check_vma=False)
```
